512 devices in a mesh: rows: 64 (over z, y), feat: 8 (over x, core).
Axes of the slice: x: 4, y: 4, z: 16, core: 2. Of those that a mesh axis runs over, the one named last changes fastest.
Arguments:
- feature_table: bfloat16 [393216, 2048], P('rows', 'feat'), may hold values from -0.21875 to 0.21875
- transition_pairs: int32 [393216, 2], P('rows'), may hold values from 0 to 6143
- task_ids: int32 [393216], P('rows'), may hold values from 0 to 63, as said below
- rewards: float32 [393216], P('rows'), may hold values from -6 to 6
Outputs:
- solution: float32 [2048, 64], P('feat')
- direction: float32 [2048, 64], P('feat')
- phi_bar: float32 [64], replicated
The draws below stay inside these ranges and needn't reach their ends.
Inputs may be any that keep to these rules, and one draw needn't show every extreme that they name: Each row indexes the 6144 states of its own block: row r uses table rows (r // 6144) * 6144 + transition_pairs[r]. `task_ids`: within each aligned block of 6144 rows every task occurs at least once.
All inputs are finite; a program needn't handle non-finite values.
Results may differ from the reference program's by a relative error of at most 0.0003.
Values sent between devices are 32-bit elements; how exact they have to be, the bound alone decides.
No kernel may reach another device: no remote copies, remote signals or barrier semaphores. Data moves between devices by JAX's collectives and lax.ppermute only.
A program may use at most 64 MiB of HBM per device.

```python
import jax
import jax.numpy as jnp
from jax import lax

F = 2048
TASKS = 64
R_DEV = 6144
ITERS = 3
ROWS = 393216
N_ROWS = 64


def draw_task_ids(key, part):
    key = jax.random.fold_in(key, 5)
    head_key, tail_key = jax.random.split(key)
    blocks = ROWS // R_DEV
    block_keys = jax.random.split(head_key, blocks)
    leading = jax.vmap(lambda sub_key: jax.random.permutation(sub_key, TASKS))(block_keys)
    trailing = jax.random.randint(tail_key, (blocks, R_DEV - TASKS), 0, TASKS)
    joined = jnp.concatenate([leading.astype(jnp.int32), trailing.astype(jnp.int32)], axis=1)
    return joined.reshape(ROWS).astype(jnp.int32)


def place_ends(array, own_key, low, high):
    place = [jax.random.randint(jax.random.fold_in(own_key, axis), (), 0, length) for axis, length in enumerate(array.shape)]
    main_axis = array.shape.index(max(array.shape))
    beside = place[:main_axis] + [(place[main_axis] + 1) % array.shape[main_axis]] + place[main_axis + 1:]
    return array.at[tuple(place)].set(low).at[tuple(beside)].set(high)


def levels(stream_key, shape, shards, least, top_value):
    factor_of, own = 1.0, jax.random.fold_in(stream_key, 6)
    for dim, parts in shards:
        heights = jnp.exp(jax.random.uniform(jax.random.fold_in(own, dim), (parts,), jnp.float32, least / len(shards), top_value / len(shards)))
        factor_of = factor_of * jnp.repeat(heights, shape[dim] // parts).reshape([-1 if axis == dim else 1 for axis in range(len(shape))])
    return factor_of


def bell_draw(own_key, extent, width, bound, shards=(), kind=jnp.bfloat16):
    factor_of = levels(own_key, extent, shards, -0.22, 0.18) if shards else 1.0
    values = jax.random.normal(own_key, extent, jnp.float32) * width * factor_of
    return jnp.minimum(jnp.maximum(values, -bound), bound).astype(kind)


def setup_inputs(seed: int = 0) -> dict:
    arg_keys = jax.random.split(jax.random.key(seed), 5)
    feature_table = bell_draw(arg_keys[0], (ROWS, F), (F * F * TASKS // ROWS) ** -0.5, 0.21875, ((0, 64), (1, 8)))
    transition_pairs = place_ends(jax.random.randint(arg_keys[1], (ROWS, 2), 0, R_DEV), jax.random.fold_in(arg_keys[1], 1), 0, R_DEV - 1).astype(jnp.int32)
    task_ids = draw_task_ids(jax.random.fold_in(arg_keys[4], 71), 0)
    rewards = bell_draw(arg_keys[3], (ROWS,), 1.0, 6.0, ((0, 64),), jnp.float32)
    return dict(feature_table=feature_table, transition_pairs=transition_pairs, task_ids=task_ids, rewards=rewards)


DISCOUNT = 0.95
PRECISE = lax.Precision.HIGHEST

def operator_block(feature_table, transition_pairs, block_index):
    offset = (block_index * R_DEV).astype(jnp.int32)
    states = lax.dynamic_slice_in_dim(feature_table, offset, R_DEV, 0)
    link_rows = lax.dynamic_slice_in_dim(transition_pairs, offset, R_DEV, 0)
    return states[link_rows[:, 0]].astype(jnp.float32) - DISCOUNT * states[link_rows[:, 1]].astype(jnp.float32)

def forward_all(feature_table, transition_pairs, onehot, right_vector):

    def one_block(block_index):
        matrix = operator_block(feature_table, transition_pairs, block_index)
        chosen = lax.dynamic_slice_in_dim(onehot, (block_index * R_DEV).astype(jnp.int32), R_DEV, 0)
        return lax.optimization_barrier(jnp.sum(jnp.dot(matrix, right_vector, precision=PRECISE) * chosen, axis=1))
    blocks = lax.map(one_block, jnp.arange(N_ROWS, dtype=jnp.int32))
    return blocks.reshape(ROWS)

def back_all(feature_table, transition_pairs, onehot, left_vector):

    def add_block(running, block_index):
        offset = (block_index * R_DEV).astype(jnp.int32)
        matrix = operator_block(feature_table, transition_pairs, block_index)
        chosen = lax.dynamic_slice_in_dim(onehot, offset, R_DEV, 0)
        values = lax.dynamic_slice_in_dim(left_vector, offset, R_DEV, 0)
        term = jnp.einsum('rf,rk->fk', matrix, chosen * values[:, None], precision=PRECISE)
        return (running + term, None)
    running, unused = lax.scan(add_block, jnp.zeros((F, TASKS), jnp.float32), jnp.arange(N_ROWS, dtype=jnp.int32))
    return running

def task_sums(onehot, values):
    return jnp.einsum('rk,r->k', onehot, values, precision=PRECISE)

def per_row(onehot, values):
    return jnp.einsum('rk,k->r', onehot, values, precision=PRECISE)

def left_normalize(onehot, raw_left):
    left_scale = jnp.sqrt(task_sums(onehot, raw_left * raw_left))
    return (raw_left * per_row(onehot, 1.0 / left_scale), left_scale)

def right_normalize(raw_right):
    right_scale = jnp.sqrt(lax.optimization_barrier(jnp.sum(raw_right * raw_right, axis=0)))
    return (raw_right / right_scale[None, :], right_scale)

def reference(feature_table, transition_pairs, task_ids, rewards):
    onehot = (task_ids[:, None] == jnp.arange(TASKS, dtype=jnp.int32)[None, :]).astype(jnp.float32)
    left_vector, left_scale = left_normalize(onehot, rewards)
    right_vector, right_scale = right_normalize(back_all(feature_table, transition_pairs, onehot, left_vector))
    direction = right_vector
    solution = jnp.zeros_like(right_vector)
    phi_bar = left_scale
    rho_bar = right_scale
    for iteration in range(ITERS):
        raw_left = forward_all(feature_table, transition_pairs, onehot, right_vector) - per_row(onehot, right_scale) * left_vector
        left_vector, left_scale = left_normalize(onehot, raw_left)
        raw_right = back_all(feature_table, transition_pairs, onehot, left_vector) - left_scale[None, :] * right_vector
        right_vector, right_scale = right_normalize(raw_right)
        rotation = jnp.sqrt(rho_bar * rho_bar + left_scale * left_scale)
        cosine = rho_bar / rotation
        sine_part = left_scale / rotation
        theta_term = sine_part * right_scale
        rho_bar = -cosine * right_scale
        phi_term = cosine * phi_bar
        phi_bar = sine_part * phi_bar
        solution = solution + (phi_term / rotation)[None, :] * direction
        direction = right_vector - (theta_term / rotation)[None, :] * direction
    return (solution, direction, phi_bar)
```

```python
import functools

import jax
import jax.numpy as jnp
from jax import lax
from jax.experimental import pallas as pl
from jax.experimental.pallas import tpu as pltpu
from jax.sharding import Mesh
from jax.sharding import PartitionSpec as P

TASKS = 64
ITERS = 3
DISCOUNT = 0.95

ROWS = 6144
FEATS = 256
GATHER = 32
CHUNK = 512
LINE = ROWS + 128

F32 = jnp.float32
BF16 = jnp.bfloat16
VMEM = pl.BlockSpec(memory_space=pltpu.VMEM)
SMEM = pl.BlockSpec(memory_space=pltpu.SMEM)


def shaped(*shape, dtype=F32):
    return jax.ShapeDtypeStruct(shape, dtype)


def call(kernel, operands, outs, scratch=(), specs=None, limit=24):
    return pl.pallas_call(
        kernel,
        out_shape=tuple(outs),
        in_specs=specs or [VMEM] * len(operands),
        out_specs=tuple([VMEM] * len(outs)),
        scratch_shapes=list(scratch),
        compiler_params=pltpu.CompilerParams(vmem_limit_bytes=limit * 2**20),
    )(*operands)


def split3(values):
    high = values.astype(BF16)
    rest = values - high.astype(F32)
    middle = rest.astype(BF16)
    low = (rest - middle.astype(F32)).astype(BF16)
    return high, middle, low


def diagonal():
    shape = (TASKS, 128)
    return lax.broadcasted_iota(jnp.int32, shape, 0) == lax.broadcasted_iota(jnp.int32, shape, 1)


def to_row(column):
    return jnp.sum(jnp.where(diagonal(), column, 0.0), axis=0, keepdims=True)


def to_column(row):
    return jnp.sum(jnp.where(diagonal(), row, 0.0), axis=1, keepdims=True)


def task_mask(task_ref, start):
    tasks = task_ref[:, pl.ds(start, CHUNK)]
    return lax.broadcasted_iota(jnp.int32, (TASKS, CHUNK), 0) == tasks


def add_back(chunk_index, mask, raw, ab_ref, acc_ref, squares):
    start = chunk_index * CHUNK
    parts = [jnp.where(mask, part.astype(F32), 0.0).astype(BF16) for part in split3(raw)]
    term = jnp.dot(
        jnp.concatenate(parts, axis=0),
        ab_ref[pl.ds(start, CHUNK), :],
        preferred_element_type=F32,
    )
    if chunk_index == 0:
        acc_ref[...] = term
    else:
        acc_ref[...] += term
    squared = jnp.where(mask, raw * raw, 0.0)
    for tile in range(CHUNK // 128):
        squares = squares + squared[:, tile * 128 : (tile + 1) * 128]
    return squares


def write_pieces(acc_ref, squares, piece_ref):
    total = acc_ref[0:64, :] + acc_ref[64:128, :] + acc_ref[128:192, :]
    back = total[:, :FEATS] - DISCOUNT * total[:, FEATS:]
    line = jnp.broadcast_to(to_row(jnp.sum(squares, axis=1, keepdims=True)), (8, 128))
    for piece in range(4):
        piece_ref[piece, 0:16, :] = back[16 * piece : 16 * piece + 16, :128]
        piece_ref[piece, 16:32, :] = back[16 * piece : 16 * piece + 16, 128:]
        piece_ref[piece, 32:40, :] = line


def start_kernel(first_ref, second_ref, table_ref, task_ref, rewards_ref, ab_ref, piece_ref, wide, left, right, acc):
    def widen(step, carry):
        base = pl.multiple_of(step * 16, 16)
        rows = table_ref[pl.ds(base, 16), :].astype(F32)
        wide[pl.ds(2 * base, 16, 2), :] = rows[:, :128]
        wide[pl.ds(2 * base + 1, 16, 2), :] = rows[:, 128:]
        return carry

    lax.fori_loop(0, ROWS // 16, widen, 0, unroll=4)

    def gather(step, carry):
        base = pl.multiple_of(step * GATHER, GATHER)
        for row in range(GATHER):
            current = pl.multiple_of(2 * first_ref[base + row], 2)
            following = pl.multiple_of(2 * second_ref[base + row], 2)
            left[2 * row : 2 * row + 2, :] = wide[pl.ds(current, 2), :]
            right[2 * row : 2 * row + 2, :] = wide[pl.ds(following, 2), :]
        for half in range(2):
            lanes = 128 * half
            ab_ref[pl.ds(base, GATHER), lanes : lanes + 128] = left[pl.ds(half, GATHER, 2), :].astype(BF16)
            ab_ref[pl.ds(base, GATHER), FEATS + lanes : FEATS + lanes + 128] = right[
                pl.ds(half, GATHER, 2), :
            ].astype(BF16)
        return carry

    lax.fori_loop(0, ROWS // GATHER, gather, 0)

    squares = jnp.zeros((TASKS, 128), F32)
    for index in range(ROWS // CHUNK):
        start = index * CHUNK
        raw = rewards_ref[:, pl.ds(start, CHUNK)]
        squares = add_back(index, task_mask(task_ref, start), raw, ab_ref, acc, squares)
    write_pieces(acc, squares, piece_ref)


def sum_kernel(copies, in_ref, out_ref):
    total = in_ref[0]
    for index in range(1, in_ref.shape[0]):
        total = total + in_ref[index]
    for index in range(copies):
        out_ref[index] = total


def raw_right_of(pieces_ref, right_ref):
    low = jnp.concatenate([pieces_ref[piece, 0:16, :] for piece in range(4)], axis=0)
    high = jnp.concatenate([pieces_ref[piece, 16:32, :] for piece in range(4)], axis=0)
    back = jnp.concatenate([low, high], axis=1)
    left_scale = jnp.sqrt(to_column(pieces_ref[0, 32:33, :]))
    raw_right = back / left_scale
    if right_ref is not None:
        raw_right = raw_right - left_scale * right_ref[...]
    return raw_right, left_scale


def forward_kernel(first, last, *refs):
    refs = list(refs)
    pieces_ref = refs.pop(0)
    right_ref = None if first else refs.pop(0)
    if last:
        line_ref, raw_ref, scale_ref = refs
    else:
        ab_ref, task_ref, line_ref, raw_ref, scale_ref = refs
    raw_right, left_scale = raw_right_of(pieces_ref, right_ref)
    raw_ref[...] = raw_right
    scale_ref[...] = jnp.broadcast_to(left_scale, (TASKS, 128))
    squares = to_row(jnp.sum(raw_right * raw_right, axis=1, keepdims=True))
    copies = line_ref.shape[0]
    if not last:
        weights = jnp.concatenate(
            [jnp.concatenate(split3(raw_right), axis=0), jnp.concatenate(split3(-DISCOUNT * raw_right), axis=0)],
            axis=1,
        )
        for index in range(ROWS // CHUNK):
            start = index * CHUNK
            product = lax.dot_general(
                weights,
                ab_ref[pl.ds(start, CHUNK), :],
                (((1,), (1,)), ((), ())),
                preferred_element_type=F32,
            )
            product = product[0:64] + product[64:128] + product[128:192]
            chosen = jnp.sum(jnp.where(task_mask(task_ref, start), product, 0.0), axis=0, keepdims=True)
            for copy in range(copies):
                line_ref[copy, :, pl.ds(start, CHUNK)] = chosen
    for copy in range(copies):
        line_ref[copy, :, pl.ds(line_ref.shape[2] - 128, 128)] = squares


def rotate(state, left_scale, right_vector, right_scale):
    solution, direction, phi_bar, rho_bar = state
    rotation = jnp.sqrt(rho_bar * rho_bar + left_scale * left_scale)
    cosine = rho_bar / rotation
    sine_part = left_scale / rotation
    theta_term = sine_part * right_scale
    rho_bar = -cosine * right_scale
    phi_term = cosine * phi_bar
    phi_bar = sine_part * phi_bar
    solution = solution + (phi_term / rotation) * direction
    direction = right_vector - (theta_term / rotation) * direction
    return (solution, direction, phi_bar, rho_bar)


def right_scale_of(line_ref):
    total = line_ref[0, :, pl.ds(line_ref.shape[2] - 128, 128)]
    for index in range(1, line_ref.shape[0]):
        total = total + line_ref[index, :, pl.ds(line_ref.shape[2] - 128, 128)]
    return jnp.sqrt(to_column(total))


def read_state(refs):
    solution, direction, phi_bar, rho_bar = refs
    return (solution[...], direction[...], phi_bar[:, 0:1], rho_bar[:, 0:1])


def back_kernel(first, *refs):
    refs = list(refs)
    line_ref, task_ref, left_ref, ab_ref, raw_ref, scale_ref = refs[:6]
    refs = refs[6:]
    old_state = None if first else read_state(refs[:4])
    refs = refs if first else refs[4:]
    piece_ref, new_left_ref, right_ref, solution_ref, direction_ref, phi_ref, rho_ref, acc = refs
    left_scale = scale_ref[:, 0:1]
    right_scale = right_scale_of(line_ref)
    right_vector = raw_ref[...] / right_scale
    by_product = 1.0 / right_scale
    by_left = right_scale / left_scale

    squares = jnp.zeros((TASKS, 128), F32)
    for index in range(ROWS // CHUNK):
        start = index * CHUNK
        product = line_ref[0, :, pl.ds(start, CHUNK)]
        for other in range(1, line_ref.shape[0]):
            product = product + line_ref[other, :, pl.ds(start, CHUNK)]
        mask = task_mask(task_ref, start)
        raw = product * jnp.sum(jnp.where(mask, by_product, 0.0), axis=0, keepdims=True)
        raw = raw - left_ref[:, pl.ds(start, CHUNK)] * jnp.sum(jnp.where(mask, by_left, 0.0), axis=0, keepdims=True)
        new_left_ref[:, pl.ds(start, CHUNK)] = raw
        squares = add_back(index, mask, raw, ab_ref, acc, squares)
    write_pieces(acc, squares, piece_ref)

    right_ref[...] = right_vector
    if first:
        state = (jnp.zeros_like(right_vector), right_vector, left_scale, right_scale)
    else:
        state = rotate(old_state, left_scale, right_vector, right_scale)
    solution_ref[...] = state[0]
    direction_ref[...] = state[1]
    phi_ref[...] = jnp.broadcast_to(state[2], (TASKS, 128))
    rho_ref[...] = jnp.broadcast_to(state[3], (TASKS, 128))


def end_kernel(line_ref, raw_ref, scale_ref, *refs):
    old_state = read_state(refs[:4])
    solution_ref, direction_ref, phi_ref = refs[4:]
    right_scale = right_scale_of(line_ref)
    state = rotate(old_state, scale_ref[:, 0:1], raw_ref[...] / right_scale, right_scale)
    solution_ref[...] = state[0].T
    direction_ref[...] = state[1].T
    phi_ref[...] = to_row(state[2])[:, :TASKS]


def exchange(array, axes):
    return lax.all_to_all(array, axes, 0, 0)


def summed(array, copies):
    return call(functools.partial(sum_kernel, copies), [array], [shaped(copies, 40, 128)], limit=8)[0]


def rows_sum(pieces, sizes):
    pieces = summed(exchange(pieces, "y"), sizes["z"])
    pieces = summed(exchange(pieces, "z"), sizes["y"])
    return exchange(pieces, "y")


def body(sizes, feature_table, transition_pairs, task_ids, rewards):
    tasks = task_ids.reshape(1, ROWS)
    left = rewards.reshape(1, ROWS)
    peers = sizes["x"] * sizes["core"]
    feat = ("x", "core")
    vectors = [shaped(TASKS, FEATS), shaped(TASKS, 128)]

    ab, pieces = call(
        start_kernel,
        [transition_pairs[:, 0], transition_pairs[:, 1], feature_table, tasks, left],
        [shaped(ROWS, 2 * FEATS, dtype=BF16), shaped(4, 40, 128)],
        scratch=[
            pltpu.VMEM((2 * ROWS, 128), F32),
            pltpu.VMEM((2 * GATHER, 128), F32),
            pltpu.VMEM((2 * GATHER, 128), F32),
            pltpu.VMEM((3 * TASKS, 2 * FEATS), F32),
        ],
        specs=[SMEM, SMEM, VMEM, VMEM, VMEM],
        limit=32,
    )
    pieces = rows_sum(pieces, sizes)
    line, raw, scale = call(
        functools.partial(forward_kernel, True, False),
        [pieces, ab, tasks],
        [shaped(peers, 1, LINE)] + vectors,
    )
    state = []
    for iteration in range(ITERS):
        line = exchange(line, feat)
        pieces, left, right, *state = call(
            functools.partial(back_kernel, iteration == 0),
            [line, tasks, left, ab, raw, scale] + state,
            [shaped(4, 40, 128), shaped(1, ROWS), shaped(TASKS, FEATS)]
            + [shaped(TASKS, FEATS)] * 2
            + [shaped(TASKS, 128)] * 2,
            scratch=[pltpu.VMEM((3 * TASKS, 2 * FEATS), F32)],
        )
        pieces = rows_sum(pieces, sizes)
        last = iteration == ITERS - 1
        line, raw, scale = call(
            functools.partial(forward_kernel, False, last),
            [pieces, right] + ([] if last else [ab, tasks]),
            [shaped(peers, 1, 128 if last else LINE)] + vectors,
        )
    line = exchange(line, feat)
    solution, direction, phi_bar = call(
        end_kernel,
        [line, raw, scale] + state,
        [shaped(FEATS, TASKS), shaped(FEATS, TASKS), shaped(1, TASKS)],
    )
    return (solution, direction, phi_bar.reshape(TASKS))


def solution(mesh):
    names = ("z", "y", "x", "core")
    grid = Mesh(mesh.devices.reshape(16, 4, 4, 2), names)
    sizes = dict(zip(names, grid.devices.shape))
    rows, feat = ("z", "y"), ("x", "core")
    return jax.shard_map(
        functools.partial(body, sizes),
        mesh=grid,
        in_specs=(P(rows, feat), P(rows, None), P(rows), P(rows)),
        out_specs=(P(feat, None), P(feat, None), P()),
        check_vma=False,
    )
```

```python
import functools

import jax
import jax.numpy as jnp
from jax import lax
from jax.experimental import pallas as pl
from jax.experimental.pallas import tpu as pltpu
from jax.sharding import Mesh
from jax.sharding import PartitionSpec as P

TASKS = 64
ITERS = 3
DISCOUNT = 0.95

ROWS = 6144
FEATS = 256
GATHER = 128
PIECES = 8
SHARE = TASKS // PIECES
CHUNK = 512
LINE = ROWS + 128

F32 = jnp.float32
BF16 = jnp.bfloat16
VMEM = pl.BlockSpec(memory_space=pltpu.VMEM)
SMEM = pl.BlockSpec(memory_space=pltpu.SMEM)


def shaped(*shape, dtype=F32):
    return jax.ShapeDtypeStruct(shape, dtype)


def call(kernel, operands, outs, scratch=(), specs=None, limit=24):
    return pl.pallas_call(
        kernel,
        out_shape=tuple(outs),
        in_specs=specs or [VMEM] * len(operands),
        out_specs=tuple([VMEM] * len(outs)),
        scratch_shapes=list(scratch),
        compiler_params=pltpu.CompilerParams(vmem_limit_bytes=limit * 2**20),
    )(*operands)


def split3(values):
    high = values.astype(BF16)
    rest = values - high.astype(F32)
    middle = rest.astype(BF16)
    low = (rest - middle.astype(F32)).astype(BF16)
    return high, middle, low


def diagonal():
    shape = (TASKS, 128)
    return lax.broadcasted_iota(jnp.int32, shape, 0) == lax.broadcasted_iota(jnp.int32, shape, 1)


def to_row(column):
    return jnp.sum(jnp.where(diagonal(), column, 0.0), axis=0, keepdims=True)


def to_column(row):
    return jnp.sum(jnp.where(diagonal(), row, 0.0), axis=1, keepdims=True)


def task_mask(task_ref, start):
    tasks = task_ref[:, pl.ds(start, CHUNK)]
    return lax.broadcasted_iota(jnp.int32, (TASKS, CHUNK), 0) == tasks


def add_back(chunk_index, mask, raw, ab_ref, acc_ref, squares):
    start = chunk_index * CHUNK
    parts = [jnp.where(mask, part.astype(F32), 0.0).astype(BF16) for part in split3(raw)]
    term = jnp.dot(
        jnp.concatenate(parts, axis=0),
        ab_ref[pl.ds(start, CHUNK), :],
        preferred_element_type=F32,
    )
    if chunk_index == 0:
        acc_ref[...] = term
    else:
        acc_ref[...] += term
    squared = jnp.where(mask, raw * raw, 0.0)
    for tile in range(CHUNK // 128):
        squares = squares + squared[:, tile * 128 : (tile + 1) * 128]
    return squares


def write_pieces(acc_ref, squares, piece_ref):
    total = acc_ref[0:64, :] + acc_ref[64:128, :] + acc_ref[128:192, :]
    back = total[:, :FEATS] - DISCOUNT * total[:, FEATS:]
    line = jnp.broadcast_to(to_row(jnp.sum(squares, axis=1, keepdims=True)), (8, 128))
    for piece in range(PIECES):
        rows = slice(SHARE * piece, SHARE * piece + SHARE)
        piece_ref[piece, 0:SHARE, :] = back[rows, :128]
        piece_ref[piece, SHARE : 2 * SHARE, :] = back[rows, 128:]
        piece_ref[piece, 2 * SHARE :, :] = line


def gather_kernel(first_ref, second_ref, table_ref, ab_ref, wide, left, right):
    def widen(step, carry):
        base = pl.multiple_of(step * 16, 16)
        rows = table_ref[pl.ds(base, 16), :].astype(F32)
        wide[pl.ds(2 * base, 16, 2), :] = rows[:, :128]
        wide[pl.ds(2 * base + 1, 16, 2), :] = rows[:, 128:]
        return carry

    lax.fori_loop(0, ROWS // 16, widen, 0, unroll=4)

    def gather(step, carry):
        base = pl.multiple_of(step * GATHER, GATHER)
        for row in range(GATHER):
            current = pl.multiple_of(first_ref[base + row], 2)
            following = pl.multiple_of(second_ref[base + row], 2)
            left[2 * row : 2 * row + 2, :] = wide[pl.ds(current, 2), :]
            right[2 * row : 2 * row + 2, :] = wide[pl.ds(following, 2), :]
        for half in range(2):
            lanes = 128 * half
            ab_ref[pl.ds(base, GATHER), lanes : lanes + 128] = left[pl.ds(half, GATHER, 2), :].astype(BF16)
            ab_ref[pl.ds(base, GATHER), FEATS + lanes : FEATS + lanes + 128] = right[
                pl.ds(half, GATHER, 2), :
            ].astype(BF16)
        return carry

    lax.fori_loop(0, ROWS // GATHER, gather, 0)


def first_back_kernel(task_ref, rewards_ref, ab_ref, piece_ref, acc):
    squares = jnp.zeros((TASKS, 128), F32)
    for index in range(ROWS // CHUNK):
        start = index * CHUNK
        raw = rewards_ref[:, pl.ds(start, CHUNK)]
        squares = add_back(index, task_mask(task_ref, start), raw, ab_ref, acc, squares)
    write_pieces(acc, squares, piece_ref)


def start(pairs, table, tasks, rewards):
    ab = call(
        gather_kernel,
        [2 * pairs[:, 0], 2 * pairs[:, 1], table],
        [shaped(ROWS, 2 * FEATS, dtype=BF16)],
        scratch=[
            pltpu.VMEM((2 * ROWS, 128), F32),
            pltpu.VMEM((2 * GATHER, 128), F32),
            pltpu.VMEM((2 * GATHER, 128), F32),
        ],
        specs=[SMEM, SMEM, VMEM],
    )[0]
    pieces = call(
        first_back_kernel,
        [tasks, rewards, ab],
        [shaped(PIECES, 24, 128)],
        scratch=[pltpu.VMEM((3 * TASKS, 2 * FEATS), F32)],
    )[0]
    return ab, pieces


def sum_kernel(copies, in_ref, out_ref):
    total = in_ref[0]
    for index in range(1, in_ref.shape[0]):
        total = total + in_ref[index]
    for index in range(copies):
        out_ref[index] = total


def raw_right_of(pieces_ref, right_ref):
    low = jnp.concatenate([pieces_ref[piece, 0:SHARE, :] for piece in range(PIECES)], axis=0)
    high = jnp.concatenate([pieces_ref[piece, SHARE : 2 * SHARE, :] for piece in range(PIECES)], axis=0)
    back = jnp.concatenate([low, high], axis=1)
    left_scale = jnp.sqrt(to_column(pieces_ref[0, 2 * SHARE : 2 * SHARE + 1, :]))
    raw_right = back / left_scale
    if right_ref is not None:
        raw_right = raw_right - left_scale * right_ref[...]
    return raw_right, left_scale


def forward_kernel(first, last, *refs):
    refs = list(refs)
    pieces_ref = refs.pop(0)
    right_ref = None if first else refs.pop(0)
    if last:
        line_ref, raw_ref, scale_ref = refs
    else:
        ab_ref, task_ref, line_ref, raw_ref, scale_ref = refs
    raw_right, left_scale = raw_right_of(pieces_ref, right_ref)
    raw_ref[...] = raw_right
    scale_ref[...] = jnp.broadcast_to(left_scale, (TASKS, 128))
    squares = to_row(jnp.sum(raw_right * raw_right, axis=1, keepdims=True))
    copies = line_ref.shape[0]
    if not last:
        weights = jnp.concatenate(
            [jnp.concatenate(split3(raw_right), axis=0), jnp.concatenate(split3(-DISCOUNT * raw_right), axis=0)],
            axis=1,
        )
        for index in range(ROWS // CHUNK):
            start = index * CHUNK
            product = lax.dot_general(
                weights,
                ab_ref[pl.ds(start, CHUNK), :],
                (((1,), (1,)), ((), ())),
                preferred_element_type=F32,
            )
            product = product[0:64] + product[64:128] + product[128:192]
            chosen = jnp.sum(jnp.where(task_mask(task_ref, start), product, 0.0), axis=0, keepdims=True)
            for copy in range(copies):
                line_ref[copy, :, pl.ds(start, CHUNK)] = chosen
    for copy in range(copies):
        line_ref[copy, :, pl.ds(line_ref.shape[2] - 128, 128)] = squares


def rotate(state, left_scale, right_vector, right_scale):
    solution, direction, phi_bar, rho_bar = state
    rotation = jnp.sqrt(rho_bar * rho_bar + left_scale * left_scale)
    cosine = rho_bar / rotation
    sine_part = left_scale / rotation
    theta_term = sine_part * right_scale
    rho_bar = -cosine * right_scale
    phi_term = cosine * phi_bar
    phi_bar = sine_part * phi_bar
    solution = solution + (phi_term / rotation) * direction
    direction = right_vector - (theta_term / rotation) * direction
    return (solution, direction, phi_bar, rho_bar)


def right_scale_of(line_ref):
    total = line_ref[0, :, pl.ds(line_ref.shape[2] - 128, 128)]
    for index in range(1, line_ref.shape[0]):
        total = total + line_ref[index, :, pl.ds(line_ref.shape[2] - 128, 128)]
    return jnp.sqrt(to_column(total))


def read_state(refs):
    solution, direction, phi_bar, rho_bar = refs
    return (solution[...], direction[...], phi_bar[:, 0:1], rho_bar[:, 0:1])


def back_kernel(first, *refs):
    refs = list(refs)
    line_ref, task_ref, left_ref, ab_ref, raw_ref, scale_ref = refs[:6]
    refs = refs[6:]
    old_state = None if first else read_state(refs[:4])
    refs = refs if first else refs[4:]
    piece_ref, new_left_ref, right_ref, solution_ref, direction_ref, phi_ref, rho_ref, acc = refs
    left_scale = scale_ref[:, 0:1]
    right_scale = right_scale_of(line_ref)
    right_vector = raw_ref[...] / right_scale
    by_product = 1.0 / right_scale
    by_left = right_scale / left_scale

    squares = jnp.zeros((TASKS, 128), F32)
    for index in range(ROWS // CHUNK):
        start = index * CHUNK
        product = line_ref[0, :, pl.ds(start, CHUNK)]
        for other in range(1, line_ref.shape[0]):
            product = product + line_ref[other, :, pl.ds(start, CHUNK)]
        mask = task_mask(task_ref, start)
        raw = product * jnp.sum(jnp.where(mask, by_product, 0.0), axis=0, keepdims=True)
        raw = raw - left_ref[:, pl.ds(start, CHUNK)] * jnp.sum(jnp.where(mask, by_left, 0.0), axis=0, keepdims=True)
        new_left_ref[:, pl.ds(start, CHUNK)] = raw
        squares = add_back(index, mask, raw, ab_ref, acc, squares)
    write_pieces(acc, squares, piece_ref)

    right_ref[...] = right_vector
    if first:
        state = (jnp.zeros_like(right_vector), right_vector, left_scale, right_scale)
    else:
        state = rotate(old_state, left_scale, right_vector, right_scale)
    solution_ref[...] = state[0]
    direction_ref[...] = state[1]
    phi_ref[...] = jnp.broadcast_to(state[2], (TASKS, 128))
    rho_ref[...] = jnp.broadcast_to(state[3], (TASKS, 128))


def end_kernel(line_ref, raw_ref, scale_ref, *refs):
    old_state = read_state(refs[:4])
    solution_ref, direction_ref, phi_ref = refs[4:]
    right_scale = right_scale_of(line_ref)
    state = rotate(old_state, scale_ref[:, 0:1], raw_ref[...] / right_scale, right_scale)
    solution_ref[...] = state[0]
    direction_ref[...] = state[1]
    phi_ref[...] = to_row(state[2])[:, :TASKS]


def exchange(array, axes):
    return lax.all_to_all(array, axes, 0, 0)


def summed(array, copies):
    return call(functools.partial(sum_kernel, copies), [array], [shaped(copies, 24, 128)], limit=8)[0]


def rows_sum(pieces, sizes):
    near, far = ("zl", "y"), "zh"
    pieces = summed(exchange(pieces, near), sizes["zh"])
    pieces = summed(exchange(pieces, far), PIECES)
    return exchange(pieces, near)


def body(sizes, feature_table, transition_pairs, task_ids, rewards):
    tasks = task_ids.reshape(1, ROWS)
    left = rewards.reshape(1, ROWS)
    peers = sizes["x"] * sizes["core"]
    feat = ("x", "core")
    vectors = [shaped(TASKS, FEATS), shaped(TASKS, 128)]

    ab, pieces = start(transition_pairs, feature_table, tasks, left)
    pieces = rows_sum(pieces, sizes)
    line, raw, scale = call(
        functools.partial(forward_kernel, True, False),
        [pieces, ab, tasks],
        [shaped(peers, 1, LINE)] + vectors,
    )
    state = []
    for iteration in range(ITERS):
        line = exchange(line, feat)
        pieces, left, right, *state = call(
            functools.partial(back_kernel, iteration == 0),
            [line, tasks, left, ab, raw, scale] + state,
            [shaped(PIECES, 24, 128), shaped(1, ROWS), shaped(TASKS, FEATS)]
            + [shaped(TASKS, FEATS)] * 2
            + [shaped(TASKS, 128)] * 2,
            scratch=[pltpu.VMEM((3 * TASKS, 2 * FEATS), F32)],
        )
        pieces = rows_sum(pieces, sizes)
        last = iteration == ITERS - 1
        line, raw, scale = call(
            functools.partial(forward_kernel, False, last),
            [pieces, right] + ([] if last else [ab, tasks]),
            [shaped(peers, 1, 128 if last else LINE)] + vectors,
        )
    line = exchange(line, feat)
    solution, direction, phi_bar = call(
        end_kernel,
        [line, raw, scale] + state,
        [shaped(TASKS, FEATS), shaped(TASKS, FEATS), shaped(1, TASKS)],
    )
    return (solution.T, direction.T, phi_bar.reshape(TASKS))


def solution(mesh):
    names = ("zh", "zl", "y", "x", "core")
    grid = Mesh(mesh.devices.reshape(8, 2, 4, 4, 2), names)
    sizes = dict(zip(names, grid.devices.shape))
    rows, feat = ("zh", "zl", "y"), ("x", "core")
    return jax.shard_map(
        functools.partial(body, sizes),
        mesh=grid,
        in_specs=(P(rows, feat), P(rows, None), P(rows), P(rows)),
        out_specs=(P(feat, None), P(feat, None), P()),
        check_vma=False,
    )
```

```python
import functools

import jax
import jax.numpy as jnp
from jax import lax
from jax.experimental import pallas as pl
from jax.experimental.pallas import tpu as pltpu
from jax.sharding import Mesh
from jax.sharding import PartitionSpec as P

TASKS = 64
ITERS = 3
DISCOUNT = 0.95

ROWS = 6144
FEATS = 256
GATHER = 128
PIECES = 8
SHARE = TASKS // PIECES
PAIRS = SHARE // 2
PIECE = (2 * PAIRS + 1, 2, 128)
CHUNK = 512
LINE = ROWS + 128

F32 = jnp.float32
BF16 = jnp.bfloat16
VMEM = pl.BlockSpec(memory_space=pltpu.VMEM)
SMEM = pl.BlockSpec(memory_space=pltpu.SMEM)


def shaped(*shape, dtype=F32):
    return jax.ShapeDtypeStruct(shape, dtype)


def call(kernel, operands, outs, scratch=(), specs=None, limit=24):
    return pl.pallas_call(
        kernel,
        out_shape=tuple(outs),
        in_specs=specs or [VMEM] * len(operands),
        out_specs=tuple([VMEM] * len(outs)),
        scratch_shapes=list(scratch),
        compiler_params=pltpu.CompilerParams(vmem_limit_bytes=limit * 2**20),
    )(*operands)


def split3(values):
    high = values.astype(BF16)
    rest = values - high.astype(F32)
    middle = rest.astype(BF16)
    low = (rest - middle.astype(F32)).astype(BF16)
    return high, middle, low


def diagonal():
    shape = (TASKS, 128)
    return lax.broadcasted_iota(jnp.int32, shape, 0) == lax.broadcasted_iota(jnp.int32, shape, 1)


def to_row(column):
    return jnp.sum(jnp.where(diagonal(), column, 0.0), axis=0, keepdims=True)


def to_column(row):
    return jnp.sum(jnp.where(diagonal(), row, 0.0), axis=1, keepdims=True)


def task_mask(task_ref, start):
    tasks = task_ref[:, pl.ds(start, CHUNK)]
    return lax.broadcasted_iota(jnp.int32, (TASKS, CHUNK), 0) == tasks


def add_back(chunk_index, mask, raw, ab_ref, acc_ref, squares):
    start = chunk_index * CHUNK
    parts = [jnp.where(mask, part.astype(F32), 0.0).astype(BF16) for part in split3(raw)]
    term = jnp.dot(
        jnp.concatenate(parts, axis=0),
        ab_ref[pl.ds(start, CHUNK), :],
        preferred_element_type=F32,
    )
    if chunk_index == 0:
        acc_ref[...] = term
    else:
        acc_ref[...] += term
    squared = jnp.where(mask, raw * raw, 0.0)
    for tile in range(CHUNK // 128):
        squares = squares + squared[:, tile * 128 : (tile + 1) * 128]
    return squares


def write_pieces(acc_ref, squares, piece_ref):
    total = acc_ref[0:64, :] + acc_ref[64:128, :] + acc_ref[128:192, :]
    back = total[:, :FEATS] - DISCOUNT * total[:, FEATS:]
    line = jnp.broadcast_to(to_row(jnp.sum(squares, axis=1, keepdims=True)), (2, 128))
    for piece in range(PIECES):
        for pair in range(PAIRS):
            row = SHARE * piece + 2 * pair
            piece_ref[piece, pair] = back[row : row + 2, :128]
            piece_ref[piece, PAIRS + pair] = back[row : row + 2, 128:]
        piece_ref[piece, 2 * PAIRS] = line


def gather_kernel(first_ref, second_ref, table_ref, ab_ref, wide, left, right):
    def widen(step, carry):
        base = pl.multiple_of(step * 16, 16)
        rows = table_ref[pl.ds(base, 16), :].astype(F32)
        wide[pl.ds(2 * base, 16, 2), :] = rows[:, :128]
        wide[pl.ds(2 * base + 1, 16, 2), :] = rows[:, 128:]
        return carry

    lax.fori_loop(0, ROWS // 16, widen, 0, unroll=4)

    def gather(step, carry):
        base = pl.multiple_of(step * GATHER, GATHER)
        for row in range(GATHER):
            current = pl.multiple_of(first_ref[base + row], 2)
            following = pl.multiple_of(second_ref[base + row], 2)
            left[2 * row : 2 * row + 2, :] = wide[pl.ds(current, 2), :]
            right[2 * row : 2 * row + 2, :] = wide[pl.ds(following, 2), :]
        for half in range(2):
            lanes = 128 * half
            ab_ref[pl.ds(base, GATHER), lanes : lanes + 128] = left[pl.ds(half, GATHER, 2), :].astype(BF16)
            ab_ref[pl.ds(base, GATHER), FEATS + lanes : FEATS + lanes + 128] = right[
                pl.ds(half, GATHER, 2), :
            ].astype(BF16)
        return carry

    lax.fori_loop(0, ROWS // GATHER, gather, 0)


def first_back_kernel(task_ref, rewards_ref, ab_ref, piece_ref, acc):
    squares = jnp.zeros((TASKS, 128), F32)
    for index in range(ROWS // CHUNK):
        start = index * CHUNK
        raw = rewards_ref[:, pl.ds(start, CHUNK)]
        squares = add_back(index, task_mask(task_ref, start), raw, ab_ref, acc, squares)
    write_pieces(acc, squares, piece_ref)


def start(pairs, table, tasks, rewards):
    ab = call(
        gather_kernel,
        [2 * pairs[:, 0], 2 * pairs[:, 1], table],
        [shaped(ROWS, 2 * FEATS, dtype=BF16)],
        scratch=[
            pltpu.VMEM((2 * ROWS, 128), F32),
            pltpu.VMEM((2 * GATHER, 128), F32),
            pltpu.VMEM((2 * GATHER, 128), F32),
        ],
        specs=[SMEM, SMEM, VMEM],
    )[0]
    pieces = call(
        first_back_kernel,
        [tasks, rewards, ab],
        [shaped(PIECES, *PIECE)],
        scratch=[pltpu.VMEM((3 * TASKS, 2 * FEATS), F32)],
    )[0]
    return ab, pieces


def sum_kernel(copies, in_ref, out_ref):
    total = in_ref[0]
    for index in range(1, in_ref.shape[0]):
        total = total + in_ref[index]
    for index in range(copies):
        out_ref[index] = total


def raw_right_of(pieces_ref, right_ref):
    low = jnp.concatenate([pieces_ref[piece, pair] for piece in range(PIECES) for pair in range(PAIRS)], axis=0)
    high = jnp.concatenate([pieces_ref[piece, PAIRS + pair] for piece in range(PIECES) for pair in range(PAIRS)], axis=0)
    back = jnp.concatenate([low, high], axis=1)
    left_scale = jnp.sqrt(to_column(pieces_ref[0, 2 * PAIRS, 0:1, :]))
    raw_right = back / left_scale
    if right_ref is not None:
        raw_right = raw_right - left_scale * right_ref[...]
    return raw_right, left_scale


def forward_kernel(first, last, *refs):
    refs = list(refs)
    pieces_ref = refs.pop(0)
    right_ref = None if first else refs.pop(0)
    if last:
        line_ref, raw_ref, scale_ref = refs
    else:
        ab_ref, task_ref, line_ref, raw_ref, scale_ref = refs
    raw_right, left_scale = raw_right_of(pieces_ref, right_ref)
    raw_ref[...] = raw_right
    scale_ref[...] = jnp.broadcast_to(left_scale, (TASKS, 128))
    squares = to_row(jnp.sum(raw_right * raw_right, axis=1, keepdims=True))
    copies = line_ref.shape[0]
    if not last:
        weights = jnp.concatenate(
            [jnp.concatenate(split3(raw_right), axis=0), jnp.concatenate(split3(-DISCOUNT * raw_right), axis=0)],
            axis=1,
        )
        for index in range(ROWS // CHUNK):
            start = index * CHUNK
            product = lax.dot_general(
                weights,
                ab_ref[pl.ds(start, CHUNK), :],
                (((1,), (1,)), ((), ())),
                preferred_element_type=F32,
            )
            product = product[0:64] + product[64:128] + product[128:192]
            chosen = jnp.sum(jnp.where(task_mask(task_ref, start), product, 0.0), axis=0, keepdims=True)
            for copy in range(copies):
                line_ref[copy, :, pl.ds(start, CHUNK)] = chosen
    for copy in range(copies):
        line_ref[copy, :, pl.ds(line_ref.shape[2] - 128, 128)] = squares


def rotate(state, left_scale, right_vector, right_scale):
    solution, direction, phi_bar, rho_bar = state
    rotation = jnp.sqrt(rho_bar * rho_bar + left_scale * left_scale)
    cosine = rho_bar / rotation
    sine_part = left_scale / rotation
    theta_term = sine_part * right_scale
    rho_bar = -cosine * right_scale
    phi_term = cosine * phi_bar
    phi_bar = sine_part * phi_bar
    solution = solution + (phi_term / rotation) * direction
    direction = right_vector - (theta_term / rotation) * direction
    return (solution, direction, phi_bar, rho_bar)


def right_scale_of(line_ref):
    total = line_ref[0, :, pl.ds(line_ref.shape[2] - 128, 128)]
    for index in range(1, line_ref.shape[0]):
        total = total + line_ref[index, :, pl.ds(line_ref.shape[2] - 128, 128)]
    return jnp.sqrt(to_column(total))


def read_state(refs):
    solution, direction, phi_bar, rho_bar = refs
    return (solution[...], direction[...], phi_bar[:, 0:1], rho_bar[:, 0:1])


def back_kernel(first, *refs):
    refs = list(refs)
    line_ref, task_ref, left_ref, ab_ref, raw_ref, scale_ref = refs[:6]
    refs = refs[6:]
    old_state = None if first else read_state(refs[:4])
    refs = refs if first else refs[4:]
    piece_ref, new_left_ref, right_ref, solution_ref, direction_ref, phi_ref, rho_ref, acc = refs
    left_scale = scale_ref[:, 0:1]
    right_scale = right_scale_of(line_ref)
    right_vector = raw_ref[...] / right_scale
    by_product = 1.0 / right_scale
    by_left = right_scale / left_scale

    squares = jnp.zeros((TASKS, 128), F32)
    for index in range(ROWS // CHUNK):
        start = index * CHUNK
        product = line_ref[0, :, pl.ds(start, CHUNK)]
        for other in range(1, line_ref.shape[0]):
            product = product + line_ref[other, :, pl.ds(start, CHUNK)]
        mask = task_mask(task_ref, start)
        raw = product * jnp.sum(jnp.where(mask, by_product, 0.0), axis=0, keepdims=True)
        raw = raw - left_ref[:, pl.ds(start, CHUNK)] * jnp.sum(jnp.where(mask, by_left, 0.0), axis=0, keepdims=True)
        new_left_ref[:, pl.ds(start, CHUNK)] = raw
        squares = add_back(index, mask, raw, ab_ref, acc, squares)
    write_pieces(acc, squares, piece_ref)

    right_ref[...] = right_vector
    if first:
        state = (jnp.zeros_like(right_vector), right_vector, left_scale, right_scale)
    else:
        state = rotate(old_state, left_scale, right_vector, right_scale)
    solution_ref[...] = state[0]
    direction_ref[...] = state[1]
    phi_ref[...] = jnp.broadcast_to(state[2], (TASKS, 128))
    rho_ref[...] = jnp.broadcast_to(state[3], (TASKS, 128))


def end_kernel(line_ref, raw_ref, scale_ref, *refs):
    old_state = read_state(refs[:4])
    solution_ref, direction_ref, phi_ref = refs[4:]
    right_scale = right_scale_of(line_ref)
    state = rotate(old_state, scale_ref[:, 0:1], raw_ref[...] / right_scale, right_scale)
    solution_ref[...] = state[0]
    direction_ref[...] = state[1]
    phi_ref[...] = to_row(state[2])[:, :TASKS]


def exchange(array, axes):
    return lax.all_to_all(array, axes, 0, 0)


def summed(array, copies):
    return call(functools.partial(sum_kernel, copies), [array], [shaped(copies, *PIECE)], limit=8)[0]


def rows_sum(pieces, sizes):
    near, far = ("zl", "y"), "zh"
    pieces = summed(exchange(pieces, near), sizes["zh"])
    pieces = summed(exchange(pieces, far), PIECES)
    return exchange(pieces, near)


def body(sizes, feature_table, transition_pairs, task_ids, rewards):
    tasks = task_ids.reshape(1, ROWS)
    left = rewards.reshape(1, ROWS)
    peers = sizes["x"] * sizes["core"]
    feat = ("x", "core")
    vectors = [shaped(TASKS, FEATS), shaped(TASKS, 128)]

    ab, pieces = start(transition_pairs, feature_table, tasks, left)
    pieces = rows_sum(pieces, sizes)
    line, raw, scale = call(
        functools.partial(forward_kernel, True, False),
        [pieces, ab, tasks],
        [shaped(peers, 1, LINE)] + vectors,
    )
    state = []
    for iteration in range(ITERS):
        line = exchange(line, feat)
        pieces, left, right, *state = call(
            functools.partial(back_kernel, iteration == 0),
            [line, tasks, left, ab, raw, scale] + state,
            [shaped(PIECES, *PIECE), shaped(1, ROWS), shaped(TASKS, FEATS)]
            + [shaped(TASKS, FEATS)] * 2
            + [shaped(TASKS, 128)] * 2,
            scratch=[pltpu.VMEM((3 * TASKS, 2 * FEATS), F32)],
        )
        pieces = rows_sum(pieces, sizes)
        last = iteration == ITERS - 1
        line, raw, scale = call(
            functools.partial(forward_kernel, False, last),
            [pieces, right] + ([] if last else [ab, tasks]),
            [shaped(peers, 1, 128 if last else LINE)] + vectors,
        )
    line = exchange(line, feat)
    solution, direction, phi_bar = call(
        end_kernel,
        [line, raw, scale] + state,
        [shaped(TASKS, FEATS), shaped(TASKS, FEATS), shaped(1, TASKS)],
    )
    return (solution.T, direction.T, phi_bar.reshape(TASKS))


def solution(mesh):
    names = ("zh", "zl", "y", "x", "core")
    grid = Mesh(mesh.devices.reshape(8, 2, 4, 4, 2), names)
    sizes = dict(zip(names, grid.devices.shape))
    rows, feat = ("zh", "zl", "y"), ("x", "core")
    return jax.shard_map(
        functools.partial(body, sizes),
        mesh=grid,
        in_specs=(P(rows, feat), P(rows, None), P(rows), P(rows)),
        out_specs=(P(feat, None), P(feat, None), P()),
        check_vma=False,
    )
```

```python
import functools

import jax
import jax.numpy as jnp
from jax import lax
from jax.experimental import pallas as pl
from jax.experimental.pallas import tpu as pltpu
from jax.sharding import Mesh
from jax.sharding import PartitionSpec as P

TASKS = 64
ITERS = 3
DISCOUNT = 0.95

ROWS = 6144
FEATS = 256
GATHER = 128
PIECES = 8
SHARE = TASKS // PIECES
PAIRS = SHARE // 2
PIECE = (2 * PAIRS + 1, 2, 128)
CHUNK = 512
LINE = ROWS + 128

F32 = jnp.float32
BF16 = jnp.bfloat16
VMEM = pl.BlockSpec(memory_space=pltpu.VMEM)
ANY = pl.BlockSpec(memory_space=pl.ANY)


def shaped(*shape, dtype=F32):
    return jax.ShapeDtypeStruct(shape, dtype)


def call(kernel, operands, outs, scratch=(), specs=None, limit=24):
    return pl.pallas_call(
        kernel,
        out_shape=tuple(outs),
        in_specs=specs or [VMEM] * len(operands),
        out_specs=tuple([VMEM] * len(outs)),
        scratch_shapes=list(scratch),
        compiler_params=pltpu.CompilerParams(vmem_limit_bytes=limit * 2**20),
    )(*operands)


def split3(values):
    high = values.astype(BF16)
    rest = values - high.astype(F32)
    middle = rest.astype(BF16)
    low = (rest - middle.astype(F32)).astype(BF16)
    return high, middle, low


def diagonal():
    shape = (TASKS, 128)
    return lax.broadcasted_iota(jnp.int32, shape, 0) == lax.broadcasted_iota(jnp.int32, shape, 1)


def to_row(column):
    return jnp.sum(jnp.where(diagonal(), column, 0.0), axis=0, keepdims=True)


def to_column(row):
    return jnp.sum(jnp.where(diagonal(), row, 0.0), axis=1, keepdims=True)


def task_mask(task_ref, start):
    tasks = task_ref[:, pl.ds(start, CHUNK)]
    return lax.broadcasted_iota(jnp.int32, (TASKS, CHUNK), 0) == tasks


def add_back(chunk_index, mask, raw, ab_ref, acc_ref, squares):
    start = chunk_index * CHUNK
    parts = [jnp.where(mask, part.astype(F32), 0.0).astype(BF16) for part in split3(raw)]
    term = jnp.dot(
        jnp.concatenate(parts, axis=0),
        ab_ref[pl.ds(start, CHUNK), :],
        preferred_element_type=F32,
    )
    if chunk_index == 0:
        acc_ref[...] = term
    else:
        acc_ref[...] += term
    squared = jnp.where(mask, raw * raw, 0.0)
    for tile in range(CHUNK // 128):
        squares = squares + squared[:, tile * 128 : (tile + 1) * 128]
    return squares


def write_pieces(acc_ref, squares, piece_ref):
    total = acc_ref[0:64, :] + acc_ref[64:128, :] + acc_ref[128:192, :]
    back = total[:, :FEATS] - DISCOUNT * total[:, FEATS:]
    line = jnp.broadcast_to(to_row(jnp.sum(squares, axis=1, keepdims=True)), (2, 128))
    for piece in range(PIECES):
        for pair in range(PAIRS):
            row = SHARE * piece + 2 * pair
            piece_ref[piece, pair] = back[row : row + 2, :128]
            piece_ref[piece, PAIRS + pair] = back[row : row + 2, 128:]
        piece_ref[piece, 2 * PAIRS] = line


def gather_kernel(first_any, second_any, table_ref, ab_ref, wide, left, right, first_ref, second_ref, sems):
    loads = [
        pltpu.make_async_copy(first_any, first_ref, sems.at[0]),
        pltpu.make_async_copy(second_any, second_ref, sems.at[1]),
    ]
    for load in loads:
        load.start()

    def widen(step, carry):
        base = pl.multiple_of(step * 16, 16)
        rows = table_ref[pl.ds(base, 16), :].astype(F32)
        wide[pl.ds(2 * base, 16, 2), :] = rows[:, :128]
        wide[pl.ds(2 * base + 1, 16, 2), :] = rows[:, 128:]
        return carry

    lax.fori_loop(0, ROWS // 16, widen, 0, unroll=4)
    for load in loads:
        load.wait()

    def fetch(chunk, buffer, first):
        base = pl.multiple_of(chunk * GATHER, GATHER)
        for row in range(first, first + 16):
            for index_ref, lines in ((first_ref, left), (second_ref, right)):
                at = pl.multiple_of(index_ref[base + row], 2)
                lines[buffer * 2 * GATHER + 2 * row : buffer * 2 * GATHER + 2 * row + 2, :] = wide[pl.ds(at, 2), :]

    def narrow(chunk, buffer, first):
        base = pl.multiple_of(chunk * GATHER + first, 16)
        for side, lines in enumerate((left, right)):
            for half in range(2):
                lanes = FEATS * side + 128 * half
                ab_ref[pl.ds(base, 16), lanes : lanes + 128] = lines[pl.ds(buffer * 2 * GATHER + 2 * first + half, 16, 2), :].astype(BF16)

    def both(chunk, buffer):
        for first in range(0, GATHER, 16):
            fetch(chunk, buffer, first)
            narrow(chunk - 1, 1 - buffer, first)

    for first in range(0, GATHER, 16):
        fetch(0, 0, first)

    def step(index, carry):
        both(2 * index + 1, 1)
        both(2 * index + 2, 0)
        return carry

    chunks = ROWS // GATHER
    lax.fori_loop(0, chunks // 2 - 1, step, 0)
    both(chunks - 1, 1)
    for first in range(0, GATHER, 16):
        narrow(chunks - 1, 1, first)


def first_back_kernel(task_ref, rewards_ref, ab_ref, piece_ref, acc):
    squares = jnp.zeros((TASKS, 128), F32)
    for index in range(ROWS // CHUNK):
        start = index * CHUNK
        raw = rewards_ref[:, pl.ds(start, CHUNK)]
        squares = add_back(index, task_mask(task_ref, start), raw, ab_ref, acc, squares)
    write_pieces(acc, squares, piece_ref)


def start(pairs, table, tasks, rewards):
    ab = call(
        gather_kernel,
        [2 * pairs[:, 0], 2 * pairs[:, 1], table],
        [shaped(ROWS, 2 * FEATS, dtype=BF16)],
        scratch=[
            pltpu.VMEM((2 * ROWS, 128), F32),
            pltpu.VMEM((4 * GATHER, 128), F32),
            pltpu.VMEM((4 * GATHER, 128), F32),
            pltpu.SMEM((ROWS,), jnp.int32),
            pltpu.SMEM((ROWS,), jnp.int32),
            pltpu.SemaphoreType.DMA((2,)),
        ],
        specs=[ANY, ANY, VMEM],
    )[0]
    pieces = call(
        first_back_kernel,
        [tasks, rewards, ab],
        [shaped(PIECES, *PIECE)],
        scratch=[pltpu.VMEM((3 * TASKS, 2 * FEATS), F32)],
    )[0]
    return ab, pieces


def sum_kernel(copies, in_ref, out_ref):
    total = in_ref[0]
    for index in range(1, in_ref.shape[0]):
        total = total + in_ref[index]
    for index in range(copies):
        out_ref[index] = total


def raw_right_of(pieces_ref, right_ref):
    low = jnp.concatenate([pieces_ref[piece, pair] for piece in range(PIECES) for pair in range(PAIRS)], axis=0)
    high = jnp.concatenate([pieces_ref[piece, PAIRS + pair] for piece in range(PIECES) for pair in range(PAIRS)], axis=0)
    back = jnp.concatenate([low, high], axis=1)
    left_scale = jnp.sqrt(to_column(pieces_ref[0, 2 * PAIRS, 0:1, :]))
    raw_right = back / left_scale
    if right_ref is not None:
        raw_right = raw_right - left_scale * right_ref[...]
    return raw_right, left_scale


def forward_kernel(first, last, *refs):
    refs = list(refs)
    pieces_ref = refs.pop(0)
    right_ref = None if first else refs.pop(0)
    if last:
        line_ref, raw_ref, scale_ref = refs
    else:
        ab_ref, task_ref, line_ref, raw_ref, scale_ref = refs
    raw_right, left_scale = raw_right_of(pieces_ref, right_ref)
    raw_ref[...] = raw_right
    scale_ref[...] = jnp.broadcast_to(left_scale, (TASKS, 128))
    squares = to_row(jnp.sum(raw_right * raw_right, axis=1, keepdims=True))
    copies = line_ref.shape[0]
    if not last:
        weights = jnp.concatenate(
            [jnp.concatenate(split3(raw_right), axis=0), jnp.concatenate(split3(-DISCOUNT * raw_right), axis=0)],
            axis=1,
        )
        for index in range(ROWS // CHUNK):
            start = index * CHUNK
            product = lax.dot_general(
                weights,
                ab_ref[pl.ds(start, CHUNK), :],
                (((1,), (1,)), ((), ())),
                preferred_element_type=F32,
            )
            product = product[0:64] + product[64:128] + product[128:192]
            chosen = jnp.sum(jnp.where(task_mask(task_ref, start), product, 0.0), axis=0, keepdims=True)
            for copy in range(copies):
                line_ref[copy, :, pl.ds(start, CHUNK)] = chosen
    for copy in range(copies):
        line_ref[copy, :, pl.ds(line_ref.shape[2] - 128, 128)] = squares


def rotate(state, left_scale, right_vector, right_scale):
    solution, direction, phi_bar, rho_bar = state
    rotation = jnp.sqrt(rho_bar * rho_bar + left_scale * left_scale)
    cosine = rho_bar / rotation
    sine_part = left_scale / rotation
    theta_term = sine_part * right_scale
    rho_bar = -cosine * right_scale
    phi_term = cosine * phi_bar
    phi_bar = sine_part * phi_bar
    solution = solution + (phi_term / rotation) * direction
    direction = right_vector - (theta_term / rotation) * direction
    return (solution, direction, phi_bar, rho_bar)


def right_scale_of(line_ref):
    total = line_ref[0, :, pl.ds(line_ref.shape[2] - 128, 128)]
    for index in range(1, line_ref.shape[0]):
        total = total + line_ref[index, :, pl.ds(line_ref.shape[2] - 128, 128)]
    return jnp.sqrt(to_column(total))


def read_state(refs):
    solution, direction, phi_bar, rho_bar = refs
    return (solution[...], direction[...], phi_bar[:, 0:1], rho_bar[:, 0:1])


def back_kernel(first, last, *refs):
    refs = list(refs)
    line_ref, task_ref, left_ref, ab_ref, raw_ref, scale_ref = refs[:6]
    refs = refs[6:]
    old_state = None if first else read_state(refs[:4])
    refs = refs if first else refs[4:]
    piece_ref, right_ref, solution_ref, direction_ref, phi_ref, rho_ref = refs[:6]
    new_left_ref = None if last else refs[6]
    acc = refs[-1]
    left_scale = scale_ref[:, 0:1]
    right_scale = right_scale_of(line_ref)
    right_vector = raw_ref[...] / right_scale
    by_product = 1.0 / right_scale
    by_left = right_scale / left_scale

    squares = jnp.zeros((TASKS, 128), F32)
    for index in range(ROWS // CHUNK):
        start = index * CHUNK
        product = line_ref[0, :, pl.ds(start, CHUNK)]
        for other in range(1, line_ref.shape[0]):
            product = product + line_ref[other, :, pl.ds(start, CHUNK)]
        mask = task_mask(task_ref, start)
        raw = product * jnp.sum(jnp.where(mask, by_product, 0.0), axis=0, keepdims=True)
        raw = raw - left_ref[:, pl.ds(start, CHUNK)] * jnp.sum(jnp.where(mask, by_left, 0.0), axis=0, keepdims=True)
        if not last:
            new_left_ref[:, pl.ds(start, CHUNK)] = raw
        squares = add_back(index, mask, raw, ab_ref, acc, squares)
    write_pieces(acc, squares, piece_ref)

    right_ref[...] = right_vector
    if first:
        state = (jnp.zeros_like(right_vector), right_vector, left_scale, right_scale)
    else:
        state = rotate(old_state, left_scale, right_vector, right_scale)
    solution_ref[...] = state[0]
    direction_ref[...] = state[1]
    phi_ref[...] = jnp.broadcast_to(state[2], (TASKS, 128))
    rho_ref[...] = jnp.broadcast_to(state[3], (TASKS, 128))


def end_kernel(line_ref, raw_ref, scale_ref, *refs):
    old_state = read_state(refs[:4])
    solution_ref, direction_ref, phi_ref = refs[4:]
    right_scale = right_scale_of(line_ref)
    state = rotate(old_state, scale_ref[:, 0:1], raw_ref[...] / right_scale, right_scale)
    solution_ref[...] = state[0]
    direction_ref[...] = state[1]
    phi_ref[...] = to_row(state[2])[:, :TASKS]


def exchange(array, axes):
    return lax.all_to_all(array, axes, 0, 0)


def summed(array, copies):
    return call(functools.partial(sum_kernel, copies), [array], [shaped(copies, *PIECE)], limit=8)[0]


def rows_sum(pieces, sizes):
    near, far = ("zl", "y"), "zh"
    pieces = summed(exchange(pieces, near), sizes["zh"])
    pieces = summed(exchange(pieces, far), PIECES)
    return exchange(pieces, near)


def body(sizes, feature_table, transition_pairs, task_ids, rewards):
    tasks = task_ids.reshape(1, ROWS)
    left = rewards.reshape(1, ROWS)
    peers = sizes["x"] * sizes["core"]
    feat = ("x", "core")
    vectors = [shaped(TASKS, FEATS), shaped(TASKS, 128)]

    ab, pieces = start(transition_pairs, feature_table, tasks, left)
    pieces = rows_sum(pieces, sizes)
    line, raw, scale = call(
        functools.partial(forward_kernel, True, False),
        [pieces, ab, tasks],
        [shaped(peers, 1, LINE)] + vectors,
    )
    state = []
    for iteration in range(ITERS):
        line = exchange(line, feat)
        last = iteration == ITERS - 1
        pieces, right, *state = call(
            functools.partial(back_kernel, iteration == 0, last),
            [line, tasks, left, ab, raw, scale] + state,
            [shaped(PIECES, *PIECE), shaped(TASKS, FEATS)]
            + [shaped(TASKS, FEATS)] * 2
            + [shaped(TASKS, 128)] * 2
            + ([] if last else [shaped(1, ROWS)]),
            scratch=[pltpu.VMEM((3 * TASKS, 2 * FEATS), F32)],
        )
        if not last:
            left = state.pop()
        pieces = rows_sum(pieces, sizes)
        line, raw, scale = call(
            functools.partial(forward_kernel, False, last),
            [pieces, right] + ([] if last else [ab, tasks]),
            [shaped(peers, 1, 128 if last else LINE)] + vectors,
        )
    line = exchange(line, feat)
    solution, direction, phi_bar = call(
        end_kernel,
        [line, raw, scale] + state,
        [shaped(TASKS, FEATS), shaped(TASKS, FEATS), shaped(1, TASKS)],
    )
    return (solution.T, direction.T, phi_bar.reshape(TASKS))


def solution(mesh):
    names = ("zh", "zl", "y", "x", "core")
    grid = Mesh(mesh.devices.reshape(8, 2, 4, 4, 2), names)
    sizes = dict(zip(names, grid.devices.shape))
    rows, feat = ("zh", "zl", "y"), ("x", "core")
    return jax.shard_map(
        functools.partial(body, sizes),
        mesh=grid,
        in_specs=(P(rows, feat), P(rows, None), P(rows), P(rows)),
        out_specs=(P(feat, None), P(feat, None), P()),
        check_vma=False,
    )
```

```python
import functools

import jax
import jax.numpy as jnp
from jax import lax
from jax.experimental import pallas as pl
from jax.experimental.pallas import tpu as pltpu
from jax.sharding import Mesh
from jax.sharding import PartitionSpec as P

TASKS = 64
ITERS = 3
DISCOUNT = 0.95

ROWS = 6144
FEATS = 256
GATHER = 128
PIECES = 8
SHARE = TASKS // PIECES
PAIRS = SHARE // 2
PIECE = (2 * PAIRS + 1, 2, 128)
CHUNK = 512
LINE = ROWS + 128

F32 = jnp.float32
BF16 = jnp.bfloat16
VMEM = pl.BlockSpec(memory_space=pltpu.VMEM)
ANY = pl.BlockSpec(memory_space=pl.ANY)


def shaped(*shape, dtype=F32):
    return jax.ShapeDtypeStruct(shape, dtype)


def call(kernel, operands, outs, scratch=(), specs=None, limit=24):
    return pl.pallas_call(
        kernel,
        out_shape=tuple(outs),
        in_specs=specs or [VMEM] * len(operands),
        out_specs=tuple([VMEM] * len(outs)),
        scratch_shapes=list(scratch),
        compiler_params=pltpu.CompilerParams(vmem_limit_bytes=limit * 2**20),
    )(*operands)


def split3(values):
    high = values.astype(BF16)
    rest = values - high.astype(F32)
    middle = rest.astype(BF16)
    low = (rest - middle.astype(F32)).astype(BF16)
    return high, middle, low


def diagonal():
    shape = (TASKS, 128)
    return lax.broadcasted_iota(jnp.int32, shape, 0) == lax.broadcasted_iota(jnp.int32, shape, 1)


def to_row(column):
    return jnp.sum(jnp.where(diagonal(), column, 0.0), axis=0, keepdims=True)


def to_column(row):
    return jnp.sum(jnp.where(diagonal(), row, 0.0), axis=1, keepdims=True)


def task_mask(task_ref, start):
    tasks = task_ref[:, pl.ds(start, CHUNK)]
    return lax.broadcasted_iota(jnp.int32, (TASKS, CHUNK), 0) == tasks


def add_back(chunk_index, mask, raw, ab_ref, acc_ref, squares):
    start = chunk_index * CHUNK
    parts = [jnp.where(mask, part.astype(F32), 0.0).astype(BF16) for part in split3(raw)]
    term = jnp.dot(
        jnp.concatenate(parts, axis=0),
        ab_ref[pl.ds(start, CHUNK), :],
        preferred_element_type=F32,
    )
    if chunk_index == 0:
        acc_ref[...] = term
    else:
        acc_ref[...] += term
    squared = jnp.where(mask, raw * raw, 0.0)
    for tile in range(CHUNK // 128):
        squares = squares + squared[:, tile * 128 : (tile + 1) * 128]
    return squares


def write_pieces(acc_ref, squares, piece_ref):
    total = acc_ref[0:64, :] + acc_ref[64:128, :] + acc_ref[128:192, :]
    back = total[:, :FEATS] - DISCOUNT * total[:, FEATS:]
    line = jnp.broadcast_to(to_row(jnp.sum(squares, axis=1, keepdims=True)), (2, 128))
    for piece in range(PIECES):
        for pair in range(PAIRS):
            row = SHARE * piece + 2 * pair
            piece_ref[piece, pair] = back[row : row + 2, :128]
            piece_ref[piece, PAIRS + pair] = back[row : row + 2, 128:]
        piece_ref[piece, 2 * PAIRS] = line


def gather_kernel(pairs_any, table_ref, ab_ref, wide, left, right, first_ref, second_ref, sems):
    loads = [
        pltpu.make_async_copy(pairs_any.at[0], first_ref, sems.at[0]),
        pltpu.make_async_copy(pairs_any.at[1], second_ref, sems.at[1]),
    ]
    for load in loads:
        load.start()

    def widen(step, carry):
        base = pl.multiple_of(step * 16, 16)
        rows = table_ref[pl.ds(base, 16), :].astype(F32)
        wide[pl.ds(2 * base, 16, 2), :] = rows[:, :128]
        wide[pl.ds(2 * base + 1, 16, 2), :] = rows[:, 128:]
        return carry

    lax.fori_loop(0, ROWS // 16, widen, 0, unroll=4)
    for load in loads:
        load.wait()

    def fetch(chunk, buffer, first):
        base = pl.multiple_of(chunk * GATHER, GATHER)
        for row in range(first, first + 8):
            for index_ref, lines in ((first_ref, left), (second_ref, right)):
                at = pl.multiple_of(index_ref[base + row], 2)
                lines[buffer * 2 * GATHER + 2 * row : buffer * 2 * GATHER + 2 * row + 2, :] = wide[pl.ds(at, 2), :]

    def narrow(chunk, buffer, first):
        base = pl.multiple_of(chunk * GATHER + first, 16)
        for side, lines in enumerate((left, right)):
            for half in range(2):
                lanes = FEATS * side + 128 * half
                ab_ref[pl.ds(base, 16), lanes : lanes + 128] = lines[pl.ds(buffer * 2 * GATHER + 2 * first + half, 16, 2), :].astype(BF16)

    def both(chunk, buffer):
        for first in range(0, GATHER, 8):
            fetch(chunk, buffer, first)
            if first % 16 == 0:
                narrow(chunk - 1, 1 - buffer, first)

    for first in range(0, GATHER, 8):
        fetch(0, 0, first)

    def step(index, carry):
        both(2 * index + 1, 1)
        both(2 * index + 2, 0)
        return carry

    chunks = ROWS // GATHER
    lax.fori_loop(0, chunks // 2 - 1, step, 0)
    both(chunks - 1, 1)
    for first in range(0, GATHER, 8):
        if first % 16 == 0:
            narrow(chunks - 1, 1, first)


def first_back_kernel(task_ref, rewards_ref, ab_ref, piece_ref, acc):
    squares = jnp.zeros((TASKS, 128), F32)
    for index in range(ROWS // CHUNK):
        start = index * CHUNK
        raw = rewards_ref[:, pl.ds(start, CHUNK)]
        squares = add_back(index, task_mask(task_ref, start), raw, ab_ref, acc, squares)
    write_pieces(acc, squares, piece_ref)


def start(pairs, table, tasks, rewards):
    ab = call(
        gather_kernel,
        [2 * pairs.T, table],
        [shaped(ROWS, 2 * FEATS, dtype=BF16)],
        scratch=[
            pltpu.VMEM((2 * ROWS, 128), F32),
            pltpu.VMEM((4 * GATHER, 128), F32),
            pltpu.VMEM((4 * GATHER, 128), F32),
            pltpu.SMEM((ROWS,), jnp.int32),
            pltpu.SMEM((ROWS,), jnp.int32),
            pltpu.SemaphoreType.DMA((2,)),
        ],
        specs=[ANY, VMEM],
    )[0]
    pieces = call(
        first_back_kernel,
        [tasks, rewards, ab],
        [shaped(PIECES, *PIECE)],
        scratch=[pltpu.VMEM((3 * TASKS, 2 * FEATS), F32)],
    )[0]
    return ab, pieces


def sum_kernel(copies, in_ref, out_ref):
    total = in_ref[0]
    for index in range(1, in_ref.shape[0]):
        total = total + in_ref[index]
    for index in range(copies):
        out_ref[index] = total


def raw_right_of(pieces_ref, right_ref):
    low = jnp.concatenate([pieces_ref[piece, pair] for piece in range(PIECES) for pair in range(PAIRS)], axis=0)
    high = jnp.concatenate([pieces_ref[piece, PAIRS + pair] for piece in range(PIECES) for pair in range(PAIRS)], axis=0)
    back = jnp.concatenate([low, high], axis=1)
    left_scale = jnp.sqrt(to_column(pieces_ref[0, 2 * PAIRS, 0:1, :]))
    raw_right = back / left_scale
    if right_ref is not None:
        raw_right = raw_right - left_scale * right_ref[...]
    return raw_right, left_scale


def forward_kernel(first, last, *refs):
    refs = list(refs)
    pieces_ref = refs.pop(0)
    right_ref = None if first else refs.pop(0)
    if last:
        line_ref, raw_ref, scale_ref = refs
    else:
        ab_ref, task_ref, line_ref, raw_ref, scale_ref = refs
    raw_right, left_scale = raw_right_of(pieces_ref, right_ref)
    raw_ref[...] = raw_right
    scale_ref[...] = jnp.broadcast_to(left_scale, (TASKS, 128))
    squares = to_row(jnp.sum(raw_right * raw_right, axis=1, keepdims=True))
    copies = line_ref.shape[0]
    if not last:
        weights = jnp.concatenate(
            [jnp.concatenate(split3(raw_right), axis=0), jnp.concatenate(split3(-DISCOUNT * raw_right), axis=0)],
            axis=1,
        )
        for index in range(ROWS // CHUNK):
            start = index * CHUNK
            product = lax.dot_general(
                weights,
                ab_ref[pl.ds(start, CHUNK), :],
                (((1,), (1,)), ((), ())),
                preferred_element_type=F32,
            )
            product = product[0:64] + product[64:128] + product[128:192]
            chosen = jnp.sum(jnp.where(task_mask(task_ref, start), product, 0.0), axis=0, keepdims=True)
            for copy in range(copies):
                line_ref[copy, :, pl.ds(start, CHUNK)] = chosen
    for copy in range(copies):
        line_ref[copy, :, pl.ds(line_ref.shape[2] - 128, 128)] = squares


def rotate(state, left_scale, right_vector, right_scale):
    solution, direction, phi_bar, rho_bar = state
    rotation = jnp.sqrt(rho_bar * rho_bar + left_scale * left_scale)
    cosine = rho_bar / rotation
    sine_part = left_scale / rotation
    theta_term = sine_part * right_scale
    rho_bar = -cosine * right_scale
    phi_term = cosine * phi_bar
    phi_bar = sine_part * phi_bar
    solution = solution + (phi_term / rotation) * direction
    direction = right_vector - (theta_term / rotation) * direction
    return (solution, direction, phi_bar, rho_bar)


def right_scale_of(line_ref):
    total = line_ref[0, :, pl.ds(line_ref.shape[2] - 128, 128)]
    for index in range(1, line_ref.shape[0]):
        total = total + line_ref[index, :, pl.ds(line_ref.shape[2] - 128, 128)]
    return jnp.sqrt(to_column(total))


def read_state(refs):
    solution, direction, phi_bar, rho_bar = refs
    return (solution[...], direction[...], phi_bar[:, 0:1], rho_bar[:, 0:1])


def back_kernel(first, last, *refs):
    refs = list(refs)
    line_ref, task_ref, left_ref, ab_ref, raw_ref, scale_ref = refs[:6]
    refs = refs[6:]
    old_state = None if first else read_state(refs[:4])
    refs = refs if first else refs[4:]
    piece_ref, right_ref, solution_ref, direction_ref, phi_ref, rho_ref = refs[:6]
    new_left_ref = None if last else refs[6]
    acc = refs[-1]
    left_scale = scale_ref[:, 0:1]
    right_scale = right_scale_of(line_ref)
    right_vector = raw_ref[...] / right_scale
    by_product = 1.0 / right_scale
    by_left = right_scale / left_scale

    squares = jnp.zeros((TASKS, 128), F32)
    for index in range(ROWS // CHUNK):
        start = index * CHUNK
        product = line_ref[0, :, pl.ds(start, CHUNK)]
        for other in range(1, line_ref.shape[0]):
            product = product + line_ref[other, :, pl.ds(start, CHUNK)]
        mask = task_mask(task_ref, start)
        raw = product * jnp.sum(jnp.where(mask, by_product, 0.0), axis=0, keepdims=True)
        raw = raw - left_ref[:, pl.ds(start, CHUNK)] * jnp.sum(jnp.where(mask, by_left, 0.0), axis=0, keepdims=True)
        if not last:
            new_left_ref[:, pl.ds(start, CHUNK)] = raw
        squares = add_back(index, mask, raw, ab_ref, acc, squares)
    write_pieces(acc, squares, piece_ref)

    right_ref[...] = right_vector
    if first:
        state = (jnp.zeros_like(right_vector), right_vector, left_scale, right_scale)
    else:
        state = rotate(old_state, left_scale, right_vector, right_scale)
    solution_ref[...] = state[0]
    direction_ref[...] = state[1]
    phi_ref[...] = jnp.broadcast_to(state[2], (TASKS, 128))
    rho_ref[...] = jnp.broadcast_to(state[3], (TASKS, 128))


def end_kernel(line_ref, raw_ref, scale_ref, *refs):
    old_state = read_state(refs[:4])
    solution_ref, direction_ref, phi_ref = refs[4:]
    right_scale = right_scale_of(line_ref)
    state = rotate(old_state, scale_ref[:, 0:1], raw_ref[...] / right_scale, right_scale)
    solution_ref[...] = state[0]
    direction_ref[...] = state[1]
    phi_ref[...] = to_row(state[2])[:, :TASKS]


def exchange(array, axes):
    return lax.all_to_all(array, axes, 0, 0)


def summed(array, copies):
    return call(functools.partial(sum_kernel, copies), [array], [shaped(copies, *PIECE)], limit=8)[0]


def rows_sum(pieces, sizes):
    near, far = ("zl", "y"), "zh"
    pieces = summed(exchange(pieces, near), sizes["zh"])
    pieces = summed(exchange(pieces, far), PIECES)
    return exchange(pieces, near)


def body(sizes, feature_table, transition_pairs, task_ids, rewards):
    tasks = task_ids.reshape(1, ROWS)
    left = rewards.reshape(1, ROWS)
    peers = sizes["x"] * sizes["core"]
    feat = ("x", "core")
    vectors = [shaped(TASKS, FEATS), shaped(TASKS, 128)]

    ab, pieces = start(transition_pairs, feature_table, tasks, left)
    pieces = rows_sum(pieces, sizes)
    line, raw, scale = call(
        functools.partial(forward_kernel, True, False),
        [pieces, ab, tasks],
        [shaped(peers, 1, LINE)] + vectors,
    )
    state = []
    for iteration in range(ITERS):
        line = exchange(line, feat)
        last = iteration == ITERS - 1
        pieces, right, *state = call(
            functools.partial(back_kernel, iteration == 0, last),
            [line, tasks, left, ab, raw, scale] + state,
            [shaped(PIECES, *PIECE), shaped(TASKS, FEATS)]
            + [shaped(TASKS, FEATS)] * 2
            + [shaped(TASKS, 128)] * 2
            + ([] if last else [shaped(1, ROWS)]),
            scratch=[pltpu.VMEM((3 * TASKS, 2 * FEATS), F32)],
        )
        if not last:
            left = state.pop()
        pieces = rows_sum(pieces, sizes)
        line, raw, scale = call(
            functools.partial(forward_kernel, False, last),
            [pieces, right] + ([] if last else [ab, tasks]),
            [shaped(peers, 1, 128 if last else LINE)] + vectors,
        )
    line = exchange(line, feat)
    solution, direction, phi_bar = call(
        end_kernel,
        [line, raw, scale] + state,
        [shaped(TASKS, FEATS), shaped(TASKS, FEATS), shaped(1, TASKS)],
    )
    return (solution.T, direction.T, phi_bar.reshape(TASKS))


def solution(mesh):
    names = ("zh", "zl", "y", "x", "core")
    grid = Mesh(mesh.devices.reshape(8, 2, 4, 4, 2), names)
    sizes = dict(zip(names, grid.devices.shape))
    rows, feat = ("zh", "zl", "y"), ("x", "core")
    return jax.shard_map(
        functools.partial(body, sizes),
        mesh=grid,
        in_specs=(P(rows, feat), P(rows, None), P(rows), P(rows)),
        out_specs=(P(feat, None), P(feat, None), P()),
        check_vma=False,
    )
```
